512 devices in a mesh: var: 8 (over z_lo, core), gx: 64 (over x, z_hi, y).
Axes of the slice: x: 4, y: 8, z: 8 (z_hi: 2, z_lo: 4; z = z_hi * 4 + z_lo), core: 2. Of those that a mesh axis runs over, the one named last changes fastest.
Arguments:
- core: bfloat16 [8, 128, 128, 128], P('var', 'gx'), may hold values from -6 to 6
- var_mix: bfloat16 [8, 8], replicated, may hold values from -2 to 2
- x_factor: bfloat16 [1024, 128], P('gx'), may hold values from -0.5 to 0.5
- y_factor: bfloat16 [1024, 128], replicated, may hold values from -0.5 to 0.5
- z_factor: bfloat16 [64, 128], replicated, may hold values from -0.5 to 0.5
Outputs:
- bricks: bfloat16 [8, 64, 64, 16, 1024], P(None, None, 'gx', 'var')
The draws below stay inside these ranges and needn't reach their ends.
All inputs are finite; a program needn't handle non-finite values.
Results may differ from the reference program's by a relative error of at most 0.0057.
Values may be sent and summed in bfloat16 or wider, within the bound.
No kernel may reach another device: no remote copies, remote signals or barrier semaphores. Data moves between devices by JAX's collectives and lax.ppermute only.
A program may use at most 64 MiB of HBM per device.

```python
import jax
import jax.numpy as jnp
from jax import lax

NV = 8
R = 128
NY = 1024
XS = 16
ZW = 64
NX = 1024
N_GX = 64


def block_scale(stream_key, shape, pieces, least, largest):
    level, own = 1.0, jax.random.fold_in(stream_key, 6)
    for dim, parts in pieces:
        steps = jnp.exp(jax.random.uniform(jax.random.fold_in(own, dim), (parts,), jnp.float32, least / len(pieces), largest / len(pieces)))
        level = level * jnp.repeat(steps, shape[dim] // parts).reshape([-1 if axis == dim else 1 for axis in range(len(shape))])
    return level


def scatter_about(rng, shape, spread, most, shards=(), dtype=jnp.bfloat16):
    drawn = spread * jax.random.normal(rng, shape, jnp.float32)
    if shards:
        drawn = drawn * block_scale(rng, shape, shards, -0.22, 0.18)
    return jnp.clip(drawn, -most, most).astype(dtype)


def setup_inputs(seed: int = 0) -> dict:
    streams_of = jax.random.split(jax.random.key(seed), 6)
    return {
        "core": scatter_about(streams_of[0], (NV, R, R, R), 1.0, 6.0, ((0, 8), (1, 64))),
        "var_mix": scatter_about(streams_of[1], (NV, NV), NV ** -0.5, 2.0),
        "x_factor": scatter_about(streams_of[2], (NX, R), R ** -0.5, 0.5, ((0, 64),)),
        "y_factor": scatter_about(streams_of[3], (NY, R), R ** -0.5, 0.5),
        "z_factor": scatter_about(streams_of[4], (ZW, R), R ** -0.5, 0.5),
    }


def reference(core, var_mix, x_factor, y_factor, z_factor):
    high = lax.Precision.HIGHEST
    part = jnp.einsum("wabc,zc->wazb", core.astype(jnp.float32), z_factor.astype(jnp.float32), precision=high)
    mixed = jnp.einsum("vw,wazb->vazb", var_mix.astype(jnp.float32), part, precision=high).astype(jnp.bfloat16)
    x_wide = x_factor.astype(jnp.float32)
    y_wide = y_factor.astype(jnp.float32)

    def rebuild(slab):
        stripe = jnp.einsum("xa,azb->xzb", x_wide, slab.astype(jnp.float32), precision=high).astype(jnp.bfloat16)
        return jnp.einsum("xzb,yb->zxy", stripe.astype(jnp.float32), y_wide, precision=high).astype(jnp.bfloat16)

    field = lax.map(rebuild, mixed)
    return field.reshape(NV, ZW, N_GX, XS, NY)
```

```python
import jax
import jax.numpy as jnp
from jax import lax
from jax.sharding import Mesh, PartitionSpec as P

VAR, COL, ROW = "var", "gx_outer", "gx_inner"
GX = (COL, ROW)


def local(core, var_mix, x_factor, y_factor, z_factor):
    high = lax.Precision.HIGHEST
    n_var, n_col, n_row = lax.axis_size(VAR), lax.axis_size(COL), lax.axis_size(ROW)
    own = core[0]
    first, rank = own.shape[0], own.shape[2]
    planes = z_factor.shape[0]
    rows = x_factor.shape[0] // n_var
    part = jnp.einsum("abc,zc->zab", own, z_factor, preferred_element_type=jnp.float32)
    lent = lax.dynamic_slice_in_dim(x_factor, lax.axis_index(VAR) * rows, rows, 0).astype(jnp.float32)
    parcel = jnp.concatenate([part, jnp.broadcast_to(lent, (planes, rows, rank))], 1)
    got = lax.all_to_all(parcel, (VAR, COL), 0, 0, tiled=True)
    got = got.reshape(n_var, n_col, first + rows, rank)
    mixed = jnp.einsum(
        "vw,wqib->viqb", var_mix.astype(jnp.float32), got[:, :, :first], precision=high
    ).astype(jnp.bfloat16)
    mixed = mixed.reshape(n_var, first * n_col, rank)
    slab = lax.all_to_all(
        jnp.broadcast_to(mixed, (n_row,) + mixed.shape), ROW, 0, 0, tiled=False
    )
    xr = got[:, :, first:].astype(jnp.bfloat16).reshape(n_var * n_col * rows, n_col, n_row, first)
    xr = xr.transpose(0, 2, 3, 1).reshape(n_var * n_col, rows, n_row, first * n_col)
    stripe = jnp.einsum("psyr,yvrb->pvsb", xr, slab, preferred_element_type=jnp.float32)
    stripe = stripe.astype(jnp.bfloat16).reshape(planes, n_var * rows, rank)
    stripe = lax.all_to_all(stripe, (VAR, COL), 0, 0, tiled=True)
    stripe = stripe.reshape(planes, n_var, rows, rank)
    out = jnp.einsum(
        "zvsb,yb->vzsy", stripe, y_factor, preferred_element_type=jnp.float32
    ).astype(jnp.bfloat16)
    return out[:, :, None]


def solution(mesh):
    n_var, n_gx = mesh.devices.shape
    fine = Mesh(mesh.devices.reshape(n_var, n_gx // 8, 8), (VAR, COL, ROW))
    placed = (P(VAR, GX, None, None), P(), P(GX, None), P(), P())
    return jax.shard_map(
        local,
        mesh=fine,
        in_specs=placed,
        out_specs=P(None, None, GX, VAR, None),
        check_vma=False,
    )
```

```python
import jax
import jax.numpy as jnp
import numpy as np
from jax import lax
from jax.sharding import Mesh, PartitionSpec as P

VAR, COL, ROW = "var", "gx_outer", "gx_inner"
GX = (COL, ROW)


def local(core, var_mix, x_factor, y_factor, z_factor):
    high = lax.Precision.HIGHEST
    n_var, n_col, n_row = lax.axis_size(VAR), lax.axis_size(COL), lax.axis_size(ROW)
    own = core[0]
    first, rank = own.shape[0], own.shape[2]
    planes = z_factor.shape[0]
    rows = x_factor.shape[0] // n_var
    part = jnp.einsum("abc,zc->zab", own, z_factor, preferred_element_type=jnp.float32)
    lent = lax.dynamic_slice_in_dim(x_factor, lax.axis_index(VAR) * rows, rows, 0).astype(jnp.float32)
    parcel = jnp.concatenate([part, jnp.broadcast_to(lent, (planes, rows, rank))], 1)
    got = lax.all_to_all(parcel, (VAR, COL), 0, 0, tiled=True)
    got = got.reshape(n_var, n_col, first + rows, rank)
    mixed = jnp.einsum(
        "vw,wqib->viqb", var_mix.astype(jnp.float32), got[:, :, :first], precision=high
    ).astype(jnp.bfloat16)
    mixed = mixed.reshape(n_var, first * n_col, rank)
    slab = lax.all_to_all(
        jnp.broadcast_to(mixed, (n_row,) + mixed.shape), ROW, 0, 0, tiled=False
    )
    source = np.arange(rank).reshape(n_col, n_row, first).transpose(1, 2, 0).reshape(-1)
    order = jnp.asarray(np.equal.outer(np.arange(rank), source), jnp.bfloat16)
    xr = got[:, :, first:].astype(jnp.bfloat16).reshape(planes * rows, rank)
    xr = jnp.dot(xr, order, preferred_element_type=jnp.float32).astype(jnp.bfloat16)
    xr = xr.reshape(planes, rows, rank)
    slab = slab.transpose(1, 0, 2, 3).reshape(n_var, rank, rank)
    stripe = jnp.einsum("psa,vab->pvsb", xr, slab, preferred_element_type=jnp.float32)
    stripe = stripe.astype(jnp.bfloat16).reshape(planes, n_var * rows, rank)
    stripe = lax.all_to_all(stripe, (VAR, COL), 0, 0, tiled=True)
    stripe = stripe.reshape(planes, n_var, rows, rank).transpose(1, 0, 2, 3)
    stripe = lax.optimization_barrier(stripe.reshape(n_var * planes * rows, rank))
    out = jnp.einsum("mb,yb->my", stripe, y_factor, preferred_element_type=jnp.float32)
    out = out.astype(jnp.bfloat16).reshape(n_var, planes, rows, y_factor.shape[0])
    return out[:, :, None]


def solution(mesh):
    n_var, n_gx = mesh.devices.shape
    fine = Mesh(mesh.devices.reshape(n_var, n_gx // 8, 8), (VAR, COL, ROW))
    placed = (P(VAR, GX, None, None), P(), P(GX, None), P(), P())
    return jax.shard_map(
        local,
        mesh=fine,
        in_specs=placed,
        out_specs=P(None, None, GX, VAR, None),
        check_vma=False,
    )
```

```python
import functools

import jax
import jax.numpy as jnp
from jax import lax
from jax.experimental import pallas as pl
from jax.experimental.pallas import tpu as pltpu
from jax.sharding import Mesh, PartitionSpec as P

VAR, COL, ROW = "var", "gx_outer", "gx_inner"
GX = (COL, ROW)
F32, BF16 = jnp.float32, jnp.bfloat16
NT = (((1,), (1,)), ((), ()))
NN = (((1,), (0,)), ((), ()))
VMEM_SPEC = pl.BlockSpec(memory_space=pltpu.VMEM)
HBM_SPEC = pl.BlockSpec(memory_space=pltpu.HBM)


def vmem(mib):
    return pltpu.CompilerParams(vmem_limit_bytes=mib << 20)


def dot(a, b, dims):
    return lax.dot_general(a, b, dims, preferred_element_type=F32)


def mix_kernel(n_col, first, got, mix, slab, xr):
    n_var = mix.shape[0]
    peers = n_var * n_col
    height = got.shape[0] // peers
    rank = got.shape[1]
    n_row = slab.shape[0]
    weights = mix[...].astype(F32)
    terms = [got[pl.ds(i, peers, stride=height), :] for i in range(first)]
    spread = [jnp.broadcast_to(weights[:, w : w + 1], (n_var, rank)) for w in range(n_var)]
    for v in range(n_var):
        sums = []
        for i in range(first):
            total = None
            for w in range(n_var):
                term = terms[i][w * n_col : (w + 1) * n_col] * spread[w][v : v + 1]
                total = term if total is None else total + term
            sums.append(total)
        block = jnp.concatenate(sums, 0).astype(BF16)
        for y in range(n_row):
            slab[y, v] = block
    to = lax.broadcasted_iota(jnp.int32, (rank, rank), 1)
    source = (to % n_col * n_row + to // (first * n_col)) * first + to // n_col % first
    order = (lax.broadcasted_iota(jnp.int32, (rank, rank), 0) == source).astype(F32).astype(BF16)
    for s in range(height - first):
        lent = got[pl.ds(first + s, peers, stride=height), :].astype(BF16)
        xr[s] = dot(lent, order, NN).astype(BF16)


def expand_kernel(stripe, y_factor, out, wide, result, packed, sem):
    planes, pairs, rank = stripe.shape
    rows = 2
    n_var = pairs // rows
    blocks = y_factor.shape[0] // rank
    height = blocks * rows
    halves = result.shape[0]
    group = n_var // halves
    wide[...] = stripe[...].astype(F32).reshape(planes * pairs, rank)
    copies = []
    for h in range(halves):
        left = jnp.concatenate(
            [
                wide[pl.ds(v * rows + s, planes, stride=pairs), :]
                for s in range(rows)
                for v in range(h * group, (h + 1) * group)
            ],
            0,
        ).astype(BF16)
        for c in range(0, blocks, 2):
            r = dot(left, y_factor[pl.ds(c * rank, 2 * rank), :], NT)
            for s in range(rows):
                for d in range(2):
                    result[h, pl.ds((c + d) * rows + s, group * planes, stride=height), :] = r[
                        s * group * planes : (s + 1) * group * planes, d * rank : (d + 1) * rank
                    ]
        for j in range(group):
            v = h * group + j
            piece = result[h, pl.ds(j * planes * height, planes * height), :]
            packed[pl.ds(v * planes, planes)] = piece.astype(BF16).reshape(planes, height, rank)
            copy = pltpu.make_async_copy(
                packed.at[pl.ds(v * planes, planes)], out.at[pl.ds(v * planes, planes)], sem.at[v]
            )
            copy.start()
            copies.append(copy)
    for copy in copies:
        copy.wait()


def local(core, var_mix, x_factor, y_factor, z_factor):
    n_var, n_col, n_row = lax.axis_size(VAR), lax.axis_size(COL), lax.axis_size(ROW)
    first, rank = core.shape[1], core.shape[3]
    planes, cells = z_factor.shape[0], y_factor.shape[0]
    rows = x_factor.shape[0] // n_var
    height = first + rows
    part = jnp.einsum("abc,zc->zab", core[0], z_factor, preferred_element_type=F32)
    lent = lax.dynamic_slice_in_dim(x_factor, lax.axis_index(VAR) * rows, rows, 0).astype(F32)
    parcel = jnp.concatenate([part, jnp.broadcast_to(lent, (planes, rows, rank))], 1)
    got = lax.all_to_all(parcel, (VAR, COL), 0, 0, tiled=True)
    slab, xr = pl.pallas_call(
        functools.partial(mix_kernel, n_col, first),
        in_specs=[VMEM_SPEC] * 2,
        out_specs=[VMEM_SPEC] * 2,
        out_shape=[
            jax.ShapeDtypeStruct((n_row, n_var, first * n_col, rank), BF16),
            jax.ShapeDtypeStruct((rows, planes, rank), BF16),
        ],
        compiler_params=vmem(4),
    )(got.reshape(planes * height, rank), var_mix)
    slab = lax.all_to_all(slab, ROW, 0, 0, tiled=True)
    slab = slab.transpose(1, 0, 2, 3).reshape(n_var, rank, rank)
    stripe = jnp.einsum("spa,vab->pvsb", xr, slab, preferred_element_type=F32)
    stripe = stripe.astype(BF16).reshape(planes, n_var * rows, rank)
    stripe = lax.all_to_all(stripe, (VAR, COL), 0, 0, tiled=True)
    blocks = cells // rank
    out = pl.pallas_call(
        expand_kernel,
        in_specs=[VMEM_SPEC] * 2,
        out_specs=HBM_SPEC,
        out_shape=jax.ShapeDtypeStruct((n_var * planes, blocks * rows, rank), BF16),
        scratch_shapes=[
            pltpu.VMEM((planes * n_var * rows, rank), F32),
            pltpu.VMEM((2, n_var // 2 * planes * blocks * rows, rank), F32),
            pltpu.VMEM((n_var * planes, blocks * rows, rank), BF16),
            pltpu.SemaphoreType.DMA((n_var,)),
        ],
        compiler_params=vmem(12),
    )(stripe, y_factor)
    out = out.reshape(n_var, planes, blocks, rows, rank).transpose(0, 1, 3, 2, 4)
    return out.reshape(n_var, planes, 1, rows, cells)


def solution(mesh):
    n_var, n_gx = mesh.devices.shape
    fine = Mesh(mesh.devices.reshape(n_var, n_gx // 8, 8), (VAR, COL, ROW))
    placed = (P(VAR, GX, None, None), P(), P(GX, None), P(), P())
    return jax.shard_map(
        local,
        mesh=fine,
        in_specs=placed,
        out_specs=P(None, None, GX, VAR, None),
        check_vma=False,
    )
```

```python
import functools

import jax
import jax.numpy as jnp
from jax import lax
from jax.experimental import pallas as pl
from jax.experimental.pallas import tpu as pltpu
from jax.sharding import Mesh, PartitionSpec as P

VAR, COL, ROW = "var", "gx_outer", "gx_inner"
GX = (COL, ROW)
F32, BF16 = jnp.float32, jnp.bfloat16
NT = (((1,), (1,)), ((), ()))
NN = (((1,), (0,)), ((), ()))
VMEM_SPEC = pl.BlockSpec(memory_space=pltpu.VMEM)
HBM_SPEC = pl.BlockSpec(memory_space=pltpu.HBM)


def vmem(mib):
    return pltpu.CompilerParams(vmem_limit_bytes=mib << 20)


def dot(a, b, dims):
    return lax.dot_general(a, b, dims, preferred_element_type=F32)


def pack_kernel(core_hbm, mix_hbm, x_hbm, z_hbm, parcel, mix_out, core, mix, xs, zs, sem):
    copies = [
        pltpu.make_async_copy(src, dst, sem.at[i])
        for i, (src, dst) in enumerate([(core_hbm, core), (z_hbm, zs), (x_hbm, xs), (mix_hbm, mix)])
    ]
    for copy in copies:
        copy.start()
    first, planes = core.shape[1], zs.shape[0]
    stripe_len = xs.shape[0]
    height = parcel.shape[0] // planes
    rows = height - first
    own = lax.axis_index(VAR) * rows
    index = lax.broadcasted_iota(jnp.int32, (rows, stripe_len), 0) + own
    picked = (lax.broadcasted_iota(jnp.int32, (rows, stripe_len), 1) == index).astype(F32).astype(BF16)
    for copy in copies:
        copy.wait()
    for i in range(first):
        parcel[pl.ds(i, planes, stride=height), :] = dot(zs[...], core[0, i], NT)
    lent = dot(picked, xs[...], NN)
    for s in range(rows):
        parcel[pl.ds(first + s, planes, stride=height), :] = jnp.broadcast_to(
            lent[s : s + 1], (planes, lent.shape[1])
        )
    mix_out[...] = mix[...].astype(F32)


def mix_kernel(n_col, first, got, mix, slab, xr):
    n_var = mix.shape[0]
    peers = n_var * n_col
    height = got.shape[0] // peers
    rank = got.shape[1]
    n_row = slab.shape[0]
    weights = mix[...]
    terms = [got[pl.ds(i, peers, stride=height), :] for i in range(first)]
    spread = [jnp.broadcast_to(weights[:, w : w + 1], (n_var, rank)) for w in range(n_var)]
    for v in range(n_var):
        sums = []
        for i in range(first):
            total = None
            for w in range(n_var):
                term = terms[i][w * n_col : (w + 1) * n_col] * spread[w][v : v + 1]
                total = term if total is None else total + term
            sums.append(total)
        block = jnp.concatenate(sums, 0).astype(BF16)
        for y in range(n_row):
            slab[y, v] = block
    to = lax.broadcasted_iota(jnp.int32, (rank, rank), 1)
    source = (to % n_col * n_row + to // (first * n_col)) * first + to // n_col % first
    order = (lax.broadcasted_iota(jnp.int32, (rank, rank), 0) == source).astype(F32).astype(BF16)
    for s in range(height - first):
        lent = got[pl.ds(first + s, peers, stride=height), :].astype(BF16)
        xr[s] = dot(lent, order, NN).astype(BF16)


def stripe_kernel(slab, xr, stripe, wide):
    n_row, n_var, share, rank = slab.shape
    rows, peers, _ = xr.shape
    height = n_var * rows
    left = xr[...].reshape(rows * peers, rank)
    for v in range(0, n_var, 2):
        right = jnp.concatenate([slab[:, v + d].reshape(n_row * share, rank) for d in range(2)], 1)
        r = dot(left, right, NN)
        for d in range(2):
            for s in range(rows):
                wide[pl.ds((v + d) * rows + s, peers, stride=height), :] = r[
                    s * peers : (s + 1) * peers, d * rank : (d + 1) * rank
                ]
    stripe[...] = wide[...].astype(BF16).reshape(peers, height, rank)


def expand_kernel(stripe, y_factor, out, wide, result, packed, sem):
    planes, pairs, rank = stripe.shape
    rows = 2
    n_var = pairs // rows
    blocks = y_factor.shape[0] // rank
    height = blocks * rows
    halves = result.shape[0]
    group = n_var // halves
    wide[...] = stripe[...].astype(F32).reshape(planes * pairs, rank)
    copies = []
    for h in range(halves):
        left = jnp.concatenate(
            [
                wide[pl.ds(v * rows + s, planes, stride=pairs), :]
                for s in range(rows)
                for v in range(h * group, (h + 1) * group)
            ],
            0,
        ).astype(BF16)
        for c in range(0, blocks, 2):
            r = dot(left, y_factor[pl.ds(c * rank, 2 * rank), :], NT)
            for s in range(rows):
                for d in range(2):
                    result[h, pl.ds((c + d) * rows + s, group * planes, stride=height), :] = r[
                        s * group * planes : (s + 1) * group * planes, d * rank : (d + 1) * rank
                    ]
        for j in range(group):
            v = h * group + j
            piece = result[h, pl.ds(j * planes * height, planes * height), :]
            packed[pl.ds(v * planes, planes)] = piece.astype(BF16).reshape(planes, height, rank)
            copy = pltpu.make_async_copy(
                packed.at[pl.ds(v * planes, planes)], out.at[pl.ds(v * planes, planes)], sem.at[v]
            )
            copy.start()
            copies.append(copy)
    for copy in copies:
        copy.wait()


def local(core, var_mix, x_factor, y_factor, z_factor):
    n_var, n_col, n_row = lax.axis_size(VAR), lax.axis_size(COL), lax.axis_size(ROW)
    first, rank = core.shape[1], core.shape[3]
    planes, cells = z_factor.shape[0], y_factor.shape[0]
    rows = x_factor.shape[0] // n_var
    height = first + rows
    parcel, mix = pl.pallas_call(
        pack_kernel,
        in_specs=[HBM_SPEC] * 4,
        out_specs=[VMEM_SPEC] * 2,
        out_shape=[pltpu.VMEM((planes * height, rank), F32), pltpu.VMEM(var_mix.shape, F32)],
        scratch_shapes=[
            pltpu.VMEM(core.shape, BF16),
            pltpu.VMEM(var_mix.shape, BF16),
            pltpu.VMEM(x_factor.shape, BF16),
            pltpu.VMEM(z_factor.shape, BF16),
            pltpu.SemaphoreType.DMA((4,)),
        ],
        compiler_params=vmem(4),
    )(*(pltpu.with_memory_space_constraint(a, pltpu.HBM) for a in (core, var_mix, x_factor, z_factor)))
    got = lax.all_to_all(parcel.reshape(planes, height, rank), (VAR, COL), 0, 0, tiled=True)
    slab, xr = pl.pallas_call(
        functools.partial(mix_kernel, n_col, first),
        in_specs=[VMEM_SPEC] * 2,
        out_specs=[VMEM_SPEC] * 2,
        out_shape=[
            jax.ShapeDtypeStruct((n_row, n_var, first * n_col, rank), BF16),
            jax.ShapeDtypeStruct((rows, planes, rank), BF16),
        ],
        compiler_params=vmem(4),
    )(got.reshape(planes * height, rank), mix)
    slab = lax.all_to_all(slab, ROW, 0, 0, tiled=True)
    stripe = pl.pallas_call(
        stripe_kernel,
        in_specs=[VMEM_SPEC] * 2,
        out_specs=VMEM_SPEC,
        out_shape=pltpu.VMEM((planes, n_var * rows, rank), BF16),
        scratch_shapes=[pltpu.VMEM((planes * n_var * rows, rank), F32)],
        compiler_params=vmem(4),
    )(slab, xr)
    stripe = lax.all_to_all(stripe, (VAR, COL), 0, 0, tiled=True)
    blocks = cells // rank
    out = pl.pallas_call(
        expand_kernel,
        in_specs=[VMEM_SPEC] * 2,
        out_specs=HBM_SPEC,
        out_shape=jax.ShapeDtypeStruct((n_var * planes, blocks * rows, rank), BF16),
        scratch_shapes=[
            pltpu.VMEM((planes * n_var * rows, rank), F32),
            pltpu.VMEM((2, n_var // 2 * planes * blocks * rows, rank), F32),
            pltpu.VMEM((n_var * planes, blocks * rows, rank), BF16),
            pltpu.SemaphoreType.DMA((n_var,)),
        ],
        compiler_params=vmem(12),
    )(stripe, y_factor)
    out = out.reshape(n_var, planes, blocks, rows, rank).transpose(0, 1, 3, 2, 4)
    return out.reshape(n_var, planes, 1, rows, cells)


def solution(mesh):
    n_var, n_gx = mesh.devices.shape
    fine = Mesh(mesh.devices.reshape(n_var, n_gx // 8, 8), (VAR, COL, ROW))
    placed = (P(VAR, GX, None, None), P(), P(GX, None), P(), P())
    return jax.shard_map(
        local,
        mesh=fine,
        in_specs=placed,
        out_specs=P(None, None, GX, VAR, None),
        check_vma=False,
    )
```

```python
import functools

import jax
import jax.numpy as jnp
from jax import lax
from jax.experimental import pallas as pl
from jax.experimental.pallas import tpu as pltpu
from jax.sharding import Mesh, PartitionSpec as P

VAR, COL, ROW = "var", "gx_outer", "gx_inner"
GX = (COL, ROW)
F32, BF16 = jnp.float32, jnp.bfloat16
NT = (((1,), (1,)), ((), ()))
NN = (((1,), (0,)), ((), ()))
VMEM_SPEC = pl.BlockSpec(memory_space=pltpu.VMEM)
HBM_SPEC = pl.BlockSpec(memory_space=pltpu.HBM)


def vmem(mib):
    return pltpu.CompilerParams(vmem_limit_bytes=mib << 20)


def dot(a, b, dims):
    return lax.dot_general(a, b, dims, preferred_element_type=F32)


def pack_kernel(core_hbm, mix_hbm, x_hbm, z_hbm, parcel, mix_out, core, mix, xs, zs, sem):
    copies = [
        pltpu.make_async_copy(src, dst, sem.at[i])
        for i, (src, dst) in enumerate([(core_hbm, core), (z_hbm, zs), (x_hbm, xs), (mix_hbm, mix)])
    ]
    for copy in copies:
        copy.start()
    first, planes = core.shape[1], zs.shape[0]
    stripe_len = xs.shape[0]
    height = parcel.shape[0] // planes
    rows = height - first
    own = lax.axis_index(VAR) * rows
    index = lax.broadcasted_iota(jnp.int32, (rows, stripe_len), 0) + own
    picked = (lax.broadcasted_iota(jnp.int32, (rows, stripe_len), 1) == index).astype(F32).astype(BF16)
    for copy in copies:
        copy.wait()
    for i in range(first):
        parcel[pl.ds(i, planes, stride=height), :] = dot(zs[...], core[0, i], NT)
    lent = dot(picked, xs[...], NN)
    for s in range(rows):
        parcel[pl.ds(first + s, planes, stride=height), :] = jnp.broadcast_to(
            lent[s : s + 1], (planes, lent.shape[1])
        )
    mix_out[...] = mix[...].astype(F32)


def mix_kernel(n_col, first, got, mix, slab, xr):
    n_var = mix.shape[0]
    peers = n_var * n_col
    height = got.shape[0] // peers
    rank = got.shape[1]
    n_row = slab.shape[0]
    weights = mix[...]
    terms = [got[pl.ds(i, peers, stride=height), :] for i in range(first)]
    spread = [jnp.broadcast_to(weights[:, w : w + 1], (n_var, rank)) for w in range(n_var)]
    for v in range(n_var):
        sums = []
        for i in range(first):
            total = None
            for w in range(n_var):
                term = terms[i][w * n_col : (w + 1) * n_col] * spread[w][v : v + 1]
                total = term if total is None else total + term
            sums.append(total)
        block = jnp.concatenate(sums, 0).astype(BF16)
        for y in range(n_row):
            slab[y, v] = block
    to = lax.broadcasted_iota(jnp.int32, (rank, rank), 1)
    source = (to % n_col * n_row + to // (first * n_col)) * first + to // n_col % first
    order = (lax.broadcasted_iota(jnp.int32, (rank, rank), 0) == source).astype(F32).astype(BF16)
    for s in range(height - first):
        lent = got[pl.ds(first + s, peers, stride=height), :].astype(BF16)
        xr[s] = dot(lent, order, NN).astype(BF16)


def stripe_kernel(slab, xr, stripe, wide):
    n_row, n_var, share, rank = slab.shape
    rows, peers, _ = xr.shape
    height = n_var * rows
    pitch = wide.shape[0] // peers
    left = xr[...].reshape(rows * peers, rank)
    for v in range(0, n_var, 2):
        right = jnp.concatenate([slab[:, v + d].reshape(n_row * share, rank) for d in range(2)], 1)
        r = dot(left, right, NN)
        for d in range(2):
            for s in range(rows):
                wide[pl.ds((v + d) * rows + s, peers, stride=pitch), :] = r[
                    s * peers : (s + 1) * peers, d * rank : (d + 1) * rank
                ]
    for p in range(peers):
        stripe[p] = wide[pl.ds(p * pitch, height), :].astype(BF16)


def expand_kernel(stripe, y_factor, out, wide, result, packed, sem):
    planes, pairs, rank = stripe.shape
    rows = 2
    n_var = pairs // rows
    blocks = y_factor.shape[0] // rank
    height = blocks * rows
    halves = result.shape[0]
    group = n_var // halves
    lead = wide.shape[0] // planes
    pitch = result.shape[1] // (group * planes)
    for p in range(planes):
        wide[pl.ds(p * lead, pairs), :] = stripe[p].astype(F32)
    copies = []
    for h in range(halves):
        left = jnp.concatenate(
            [
                wide[pl.ds(v * rows + s, planes, stride=lead), :]
                for s in range(rows)
                for v in range(h * group, (h + 1) * group)
            ],
            0,
        ).astype(BF16)
        for c in range(0, blocks, 2):
            r = dot(left, y_factor[pl.ds(c * rank, 2 * rank), :], NT)
            for s in range(rows):
                for d in range(2):
                    result[h, pl.ds((c + d) * rows + s, group * planes, stride=pitch), :] = r[
                        s * group * planes : (s + 1) * group * planes, d * rank : (d + 1) * rank
                    ]
        for j in range(group):
            v = h * group + j
            for p in range(planes):
                piece = result[h, pl.ds((j * planes + p) * pitch, height), :]
                packed[v * planes + p] = piece.astype(BF16)
            copy = pltpu.make_async_copy(
                packed.at[pl.ds(v * planes, planes)], out.at[pl.ds(v * planes, planes)], sem.at[v]
            )
            copy.start()
            copies.append(copy)
    for copy in copies:
        copy.wait()


def local(core, var_mix, x_factor, y_factor, z_factor):
    n_var, n_col, n_row = lax.axis_size(VAR), lax.axis_size(COL), lax.axis_size(ROW)
    first, rank = core.shape[1], core.shape[3]
    planes, cells = z_factor.shape[0], y_factor.shape[0]
    rows = x_factor.shape[0] // n_var
    height = first + rows
    parcel, mix = pl.pallas_call(
        pack_kernel,
        in_specs=[HBM_SPEC] * 4,
        out_specs=[VMEM_SPEC] * 2,
        out_shape=[pltpu.VMEM((planes * height, rank), F32), pltpu.VMEM(var_mix.shape, F32)],
        scratch_shapes=[
            pltpu.VMEM(core.shape, BF16),
            pltpu.VMEM(var_mix.shape, BF16),
            pltpu.VMEM(x_factor.shape, BF16),
            pltpu.VMEM(z_factor.shape, BF16),
            pltpu.SemaphoreType.DMA((4,)),
        ],
        compiler_params=vmem(4),
    )(*(pltpu.with_memory_space_constraint(a, pltpu.HBM) for a in (core, var_mix, x_factor, z_factor)))
    got = lax.all_to_all(parcel.reshape(planes, height, rank), (VAR, COL), 0, 0, tiled=True)
    slab, xr = pl.pallas_call(
        functools.partial(mix_kernel, n_col, first),
        in_specs=[VMEM_SPEC] * 2,
        out_specs=[VMEM_SPEC] * 2,
        out_shape=[
            jax.ShapeDtypeStruct((n_row, n_var, first * n_col, rank), BF16),
            jax.ShapeDtypeStruct((rows, planes, rank), BF16),
        ],
        compiler_params=vmem(4),
    )(got.reshape(planes * height, rank), mix)
    slab = lax.all_to_all(slab, ROW, 0, 0, tiled=True)
    stripe = pl.pallas_call(
        stripe_kernel,
        in_specs=[VMEM_SPEC] * 2,
        out_specs=VMEM_SPEC,
        out_shape=pltpu.VMEM((planes, n_var * rows, rank), BF16),
        scratch_shapes=[pltpu.VMEM((planes * (n_var * rows + 1), rank), F32)],
        compiler_params=vmem(4),
    )(slab, xr)
    stripe = lax.all_to_all(stripe, (VAR, COL), 0, 0, tiled=True)
    blocks = cells // rank
    out = pl.pallas_call(
        expand_kernel,
        in_specs=[VMEM_SPEC] * 2,
        out_specs=HBM_SPEC,
        out_shape=jax.ShapeDtypeStruct((n_var * planes, blocks * rows, rank), BF16),
        scratch_shapes=[
            pltpu.VMEM((planes * (n_var * rows + 1), rank), F32),
            pltpu.VMEM((n_var // 2, 2 * planes * (blocks * rows + 1), rank), F32),
            pltpu.VMEM((n_var * planes, blocks * rows, rank), BF16),
            pltpu.SemaphoreType.DMA((n_var,)),
        ],
        compiler_params=vmem(12),
    )(stripe, y_factor)
    out = out.reshape(n_var, planes, blocks, rows, rank).transpose(0, 1, 3, 2, 4)
    return out.reshape(n_var, planes, 1, rows, cells)


def solution(mesh):
    n_var, n_gx = mesh.devices.shape
    fine = Mesh(mesh.devices.reshape(n_var, n_gx // 8, 8), (VAR, COL, ROW))
    placed = (P(VAR, GX, None, None), P(), P(GX, None), P(), P())
    return jax.shard_map(
        local,
        mesh=fine,
        in_specs=placed,
        out_specs=P(None, None, GX, VAR, None),
        check_vma=False,
    )
```

```python
import functools

import jax
import jax.numpy as jnp
from jax import lax
from jax.experimental import pallas as pl
from jax.experimental.pallas import tpu as pltpu
from jax.sharding import Mesh, PartitionSpec as P

SLOW, CORE, COL, ROW = "var_outer", "var_inner", "gx_outer", "gx_inner"
VAR, GX = (SLOW, CORE), (COL, ROW)
F32, BF16 = jnp.float32, jnp.bfloat16
NT = (((1,), (1,)), ((), ()))
NN = (((1,), (0,)), ((), ()))
VMEM_SPEC = pl.BlockSpec(memory_space=pltpu.VMEM)
HBM_SPEC = pl.BlockSpec(memory_space=pltpu.HBM)


def vmem(mib):
    return pltpu.CompilerParams(vmem_limit_bytes=mib << 20)


def dot(a, b, dims):
    return lax.dot_general(a, b, dims, preferred_element_type=F32)


def pack_kernel(n_slow, core_hbm, mix_hbm, x_hbm, z_hbm, parcel, mix_out, core, mix, xs, zs, sem):
    copies = [
        pltpu.make_async_copy(src, dst, sem.at[i])
        for i, (src, dst) in enumerate([(core_hbm, core), (z_hbm, zs), (x_hbm, xs), (mix_hbm, mix)])
    ]
    for copy in copies:
        copy.start()
    first, planes = core.shape[1], zs.shape[0]
    run = planes // n_slow
    stripe_len, rank = xs.shape
    own = lax.axis_index(SLOW) * first * first + lax.axis_index(CORE)
    index = lax.broadcasted_iota(jnp.int32, (first, stripe_len), 0) * first + own
    picked = (lax.broadcasted_iota(jnp.int32, (first, stripe_len), 1) == index).astype(F32).astype(BF16)
    for copy in copies:
        copy.wait()
    lent = dot(picked, xs[...], NN)
    for d in range(first):
        part = dot(zs[...], core[0, d], NT)
        row = jnp.broadcast_to(lent[d : d + 1], (run, rank))
        for t in range(n_slow):
            start = (t * first + d) * run * 2
            parcel[pl.ds(start, run, stride=2), :] = part[t * run : (t + 1) * run]
            parcel[pl.ds(start + 1, run, stride=2), :] = row
    mix_out[...] = mix[...].astype(F32)


def mix_kernel(n_slow, got, mix, slab, xr):
    n_var = mix.shape[0]
    peers, rank = got.shape[0] // 2, got.shape[1]
    run = peers // n_var
    rows = n_var // n_slow
    weights = mix[...]
    terms = got[pl.ds(0, peers, stride=2), :]
    for v in range(n_var):
        total = None
        for w in range(n_var):
            weight = jnp.broadcast_to(weights[v : v + 1, w : w + 1], (run, rank))
            term = terms[w * run : (w + 1) * run] * weight
            total = term if total is None else total + term
        block = total.astype(BF16)
        for p in range(slab.shape[0]):
            slab[p, v] = block
    half = rank // rows
    to = lax.broadcasted_iota(jnp.int32, (rank, rank), 1)
    source = to % half * rows + to // half
    order = (lax.broadcasted_iota(jnp.int32, (rank, rank), 0) == source).astype(F32).astype(BF16)
    lent = got[pl.ds(1, peers, stride=2), :].astype(BF16)
    lent = dot(lent, order, NN).astype(BF16)
    for t in range(n_slow):
        for s in range(rows):
            start = (t * rows + s) * run
            xr[s, pl.ds(t * run, run)] = lent[start : start + run]


def stripe_kernel(slab, xr, stripe, wide):
    n_row, n_var, share, rank = slab.shape
    rows, peers, _ = xr.shape
    height = n_var * rows
    pitch = wide.shape[0] // peers
    left = xr[...].reshape(rows * peers, rank)
    for v in range(0, n_var, 2):
        right = jnp.concatenate([slab[:, v + d].reshape(n_row * share, rank) for d in range(2)], 1)
        r = dot(left, right, NN)
        for d in range(2):
            for s in range(rows):
                wide[pl.ds((v + d) * rows + s, peers, stride=pitch), :] = r[
                    s * peers : (s + 1) * peers, d * rank : (d + 1) * rank
                ]
    for p in range(peers):
        stripe[p] = wide[pl.ds(p * pitch, height), :].astype(BF16)


def expand_kernel(stripe, y_factor, out, wide, result, packed, sem):
    planes, pairs, rank = stripe.shape
    rows = 2
    n_var = pairs // rows
    blocks = y_factor.shape[0] // rank
    height = blocks * rows
    halves = result.shape[0]
    group = n_var // halves
    lead = wide.shape[0] // planes
    pitch = result.shape[1] // (group * planes)
    for p in range(planes):
        wide[pl.ds(p * lead, pairs), :] = stripe[p].astype(F32)
    copies = []
    for h in range(halves):
        left = jnp.concatenate(
            [
                wide[pl.ds(v * rows + s, planes, stride=lead), :]
                for s in range(rows)
                for v in range(h * group, (h + 1) * group)
            ],
            0,
        ).astype(BF16)
        for c in range(0, blocks, 2):
            r = dot(left, y_factor[pl.ds(c * rank, 2 * rank), :], NT)
            for s in range(rows):
                for d in range(2):
                    result[h, pl.ds((c + d) * rows + s, group * planes, stride=pitch), :] = r[
                        s * group * planes : (s + 1) * group * planes, d * rank : (d + 1) * rank
                    ]
        for j in range(group):
            v = h * group + j
            for p in range(planes):
                piece = result[h, pl.ds((j * planes + p) * pitch, height), :]
                packed[v * planes + p] = piece.astype(BF16)
            copy = pltpu.make_async_copy(
                packed.at[pl.ds(v * planes, planes)], out.at[pl.ds(v * planes, planes)], sem.at[v]
            )
            copy.start()
            copies.append(copy)
    for copy in copies:
        copy.wait()


def local(core, var_mix, x_factor, y_factor, z_factor):
    n_slow, n_core, n_col = lax.axis_size(SLOW), lax.axis_size(CORE), lax.axis_size(COL)
    n_var = n_slow * n_core
    rank = core.shape[3]
    planes, cells = z_factor.shape[0], y_factor.shape[0]
    rows = x_factor.shape[0] // n_var
    assert core.shape[1] == n_core == rows
    peers = planes * n_core
    parcel, mix = pl.pallas_call(
        functools.partial(pack_kernel, n_slow),
        in_specs=[HBM_SPEC] * 4,
        out_specs=[VMEM_SPEC] * 2,
        out_shape=[pltpu.VMEM((peers * 2, rank), F32), pltpu.VMEM(var_mix.shape, F32)],
        scratch_shapes=[
            pltpu.VMEM(core.shape, BF16),
            pltpu.VMEM(var_mix.shape, BF16),
            pltpu.VMEM(x_factor.shape, BF16),
            pltpu.VMEM(z_factor.shape, BF16),
            pltpu.SemaphoreType.DMA((4,)),
        ],
        compiler_params=vmem(4),
    )(*(pltpu.with_memory_space_constraint(a, pltpu.HBM) for a in (core, var_mix, x_factor, z_factor)))
    got = lax.all_to_all(parcel.reshape(peers, 2, rank), (SLOW, CORE, ROW), 0, 0, tiled=True)
    slab, xr = pl.pallas_call(
        functools.partial(mix_kernel, n_slow),
        in_specs=[VMEM_SPEC] * 2,
        out_specs=[VMEM_SPEC] * 2,
        out_shape=[
            jax.ShapeDtypeStruct((n_core * n_col, n_var, peers // n_var, rank), BF16),
            jax.ShapeDtypeStruct((rows, planes, rank), BF16),
        ],
        compiler_params=vmem(4),
    )(got.reshape(peers * 2, rank), mix)
    slab = lax.all_to_all(slab, (CORE, COL), 0, 0, tiled=True)
    stripe = pl.pallas_call(
        stripe_kernel,
        in_specs=[VMEM_SPEC] * 2,
        out_specs=VMEM_SPEC,
        out_shape=pltpu.VMEM((planes, n_var * rows, rank), BF16),
        scratch_shapes=[pltpu.VMEM((planes * (n_var * rows + 1), rank), F32)],
        compiler_params=vmem(4),
    )(slab, xr)
    stripe = lax.all_to_all(stripe, (SLOW, ROW), 0, 0, tiled=True)
    blocks = cells // rank
    out = pl.pallas_call(
        expand_kernel,
        in_specs=[VMEM_SPEC] * 2,
        out_specs=HBM_SPEC,
        out_shape=jax.ShapeDtypeStruct((n_var * planes, blocks * rows, rank), BF16),
        scratch_shapes=[
            pltpu.VMEM((planes * (n_var * rows + 1), rank), F32),
            pltpu.VMEM((n_var // 2, 2 * planes * (blocks * rows + 1), rank), F32),
            pltpu.VMEM((n_var * planes, blocks * rows, rank), BF16),
            pltpu.SemaphoreType.DMA((n_var,)),
        ],
        compiler_params=vmem(12),
    )(stripe, y_factor)
    out = out.reshape(n_var, planes, blocks, rows, rank).transpose(0, 1, 3, 2, 4)
    return out.reshape(n_var, planes, 1, rows, cells)


def solution(mesh):
    n_var, n_gx = mesh.devices.shape
    fine = Mesh(mesh.devices.reshape(n_var // 2, 2, n_gx // 16, 16), (SLOW, CORE, COL, ROW))
    placed = (P(VAR, GX, None, None), P(), P(GX, None), P(), P())
    return jax.shard_map(
        local,
        mesh=fine,
        in_specs=placed,
        out_specs=P(None, None, GX, VAR, None),
        check_vma=False,
    )
```

```python
import functools

import jax
import jax.numpy as jnp
from jax import lax
from jax.experimental import pallas as pl
from jax.experimental.pallas import tpu as pltpu
from jax.sharding import Mesh, PartitionSpec as P

SLOW, CORE, COL, ROW = "var_outer", "var_inner", "gx_outer", "gx_inner"
VAR, GX = (SLOW, CORE), (COL, ROW)
F32, BF16 = jnp.float32, jnp.bfloat16
NT = (((1,), (1,)), ((), ()))
NN = (((1,), (0,)), ((), ()))
VMEM_SPEC = pl.BlockSpec(memory_space=pltpu.VMEM)
HBM_SPEC = pl.BlockSpec(memory_space=pltpu.HBM)


def vmem(mib):
    return pltpu.CompilerParams(vmem_limit_bytes=mib << 20)


def dot(a, b, dims):
    return lax.dot_general(a, b, dims, preferred_element_type=F32)


def pack_kernel(both, mix_hbm, x_hbm, z_hbm, parcel, mix_out, mix, xs, zs, sem):
    copies = [
        pltpu.make_async_copy(src, dst, sem.at[i])
        for i, (src, dst) in enumerate([(z_hbm, zs), (x_hbm, xs), (mix_hbm, mix)])
    ]
    for copy in copies:
        copy.start()
    n_core, planes = both.shape[0], zs.shape[0]
    stripe_len, rank = xs.shape
    height = parcel.shape[0] // planes
    rows = height - n_core
    mode = lax.axis_index(CORE)
    own = (lax.axis_index(SLOW) * n_core + mode) * rows
    index = lax.broadcasted_iota(jnp.int32, (rows, stripe_len), 0) + own
    picked = (lax.broadcasted_iota(jnp.int32, (rows, stripe_len), 1) == index).astype(F32).astype(BF16)
    for copy in copies:
        copy.wait()
    lent = dot(picked, xs[...], NN)
    for d in range(n_core):
        parcel[pl.ds(d, planes, stride=height), :] = dot(zs[...], both[d, mode], NT)
    for s in range(rows):
        row = jnp.broadcast_to(lent[s : s + 1], (planes, rank))
        parcel[pl.ds(n_core + s, planes, stride=height), :] = row
    mix_out[...] = mix[...].astype(F32)


def mix_kernel(n_slow, got, mix, slab, xr):
    n_var = mix.shape[0]
    n_core = n_var // n_slow
    rows, peers, rank = xr.shape
    height = n_core + rows
    run = peers // n_slow
    weights = mix[...]
    terms = [got[pl.ds(d, peers, stride=height), :] for d in range(n_core)]
    for v in range(n_var):
        total = None
        for w in range(n_var):
            weight = jnp.broadcast_to(weights[v : v + 1, w : w + 1], (run, rank))
            t = w // n_core
            term = terms[w % n_core][t * run : (t + 1) * run] * weight
            total = term if total is None else total + term
        block = total.astype(BF16)
        for p in range(slab.shape[0]):
            slab[p, v] = block
    half = rank // rows
    to = lax.broadcasted_iota(jnp.int32, (rank, rank), 1)
    source = to % half * rows + to // half
    order = (lax.broadcasted_iota(jnp.int32, (rank, rank), 0) == source).astype(F32).astype(BF16)
    for s in range(rows):
        lent = got[pl.ds(n_core + s, peers, stride=height), :].astype(BF16)
        xr[s] = dot(lent, order, NN).astype(BF16)


def stripe_kernel(slab, xr, stripe, wide):
    n_row, n_var, share, rank = slab.shape
    rows, peers, _ = xr.shape
    height = n_var * rows
    pitch = wide.shape[0] // peers
    left = xr[...].reshape(rows * peers, rank)
    for v in range(0, n_var, 2):
        right = jnp.concatenate([slab[:, v + d].reshape(n_row * share, rank) for d in range(2)], 1)
        r = dot(left, right, NN)
        for d in range(2):
            for s in range(rows):
                wide[pl.ds((v + d) * rows + s, peers, stride=pitch), :] = r[
                    s * peers : (s + 1) * peers, d * rank : (d + 1) * rank
                ]
    for p in range(peers):
        stripe[p] = wide[pl.ds(p * pitch, height), :].astype(BF16)


def expand_kernel(stripe, y_factor, out, wide, result, packed, sem):
    planes, pairs, rank = stripe.shape
    rows = 2
    n_var = pairs // rows
    blocks = y_factor.shape[0] // rank
    height = blocks * rows
    halves = result.shape[0]
    group = n_var // halves
    lead = wide.shape[0] // planes
    pitch = result.shape[1] // (group * planes)
    for p in range(planes):
        wide[pl.ds(p * lead, pairs), :] = stripe[p].astype(F32)
    copies = []
    for h in range(halves):
        left = jnp.concatenate(
            [
                wide[pl.ds(v * rows + s, planes, stride=lead), :]
                for s in range(rows)
                for v in range(h * group, (h + 1) * group)
            ],
            0,
        ).astype(BF16)
        for c in range(0, blocks, 2):
            r = dot(left, y_factor[pl.ds(c * rank, 2 * rank), :], NT)
            for s in range(rows):
                for d in range(2):
                    result[h, pl.ds((c + d) * rows + s, group * planes, stride=pitch), :] = r[
                        s * group * planes : (s + 1) * group * planes, d * rank : (d + 1) * rank
                    ]
        for j in range(group):
            v = h * group + j
            for p in range(planes):
                piece = result[h, pl.ds((j * planes + p) * pitch, height), :]
                packed[v * planes + p] = piece.astype(BF16)
            copy = pltpu.make_async_copy(
                packed.at[pl.ds(v * planes, planes)], out.at[pl.ds(v * planes, planes)], sem.at[v]
            )
            copy.start()
            copies.append(copy)
    for copy in copies:
        copy.wait()


def local(core, var_mix, x_factor, y_factor, z_factor):
    n_slow, n_core, n_col = lax.axis_size(SLOW), lax.axis_size(CORE), lax.axis_size(COL)
    n_var = n_slow * n_core
    rank = core.shape[3]
    planes, cells = z_factor.shape[0], y_factor.shape[0]
    rows = x_factor.shape[0] // n_var
    assert core.shape[1] == n_core
    height = n_core + rows
    both = lax.all_gather(core[0], CORE)
    parcel, mix = pl.pallas_call(
        pack_kernel,
        in_specs=[VMEM_SPEC] + [HBM_SPEC] * 3,
        out_specs=[VMEM_SPEC] * 2,
        out_shape=[pltpu.VMEM((planes * height, rank), F32), pltpu.VMEM(var_mix.shape, F32)],
        scratch_shapes=[
            pltpu.VMEM(var_mix.shape, BF16),
            pltpu.VMEM(x_factor.shape, BF16),
            pltpu.VMEM(z_factor.shape, BF16),
            pltpu.SemaphoreType.DMA((3,)),
        ],
        compiler_params=vmem(4),
    )(both, *(pltpu.with_memory_space_constraint(a, pltpu.HBM) for a in (var_mix, x_factor, z_factor)))
    got = lax.all_to_all(parcel.reshape(planes, height, rank), (SLOW, ROW), 0, 0, tiled=True)
    slab, xr = pl.pallas_call(
        functools.partial(mix_kernel, n_slow),
        in_specs=[VMEM_SPEC] * 2,
        out_specs=[VMEM_SPEC] * 2,
        out_shape=[
            jax.ShapeDtypeStruct((n_core * n_col, n_var, planes // n_slow, rank), BF16),
            jax.ShapeDtypeStruct((rows, planes, rank), BF16),
        ],
        compiler_params=vmem(4),
    )(got.reshape(planes * height, rank), mix)
    slab = lax.all_to_all(slab, (CORE, COL), 0, 0, tiled=True)
    stripe = pl.pallas_call(
        stripe_kernel,
        in_specs=[VMEM_SPEC] * 2,
        out_specs=VMEM_SPEC,
        out_shape=pltpu.VMEM((planes, n_var * rows, rank), BF16),
        scratch_shapes=[pltpu.VMEM((planes * (n_var * rows + 1), rank), F32)],
        compiler_params=vmem(4),
    )(slab, xr)
    stripe = lax.all_to_all(stripe, (SLOW, ROW), 0, 0, tiled=True)
    blocks = cells // rank
    out = pl.pallas_call(
        expand_kernel,
        in_specs=[VMEM_SPEC] * 2,
        out_specs=HBM_SPEC,
        out_shape=jax.ShapeDtypeStruct((n_var * planes, blocks * rows, rank), BF16),
        scratch_shapes=[
            pltpu.VMEM((planes * (n_var * rows + 1), rank), F32),
            pltpu.VMEM((n_var // 2, 2 * planes * (blocks * rows + 1), rank), F32),
            pltpu.VMEM((n_var * planes, blocks * rows, rank), BF16),
            pltpu.SemaphoreType.DMA((n_var,)),
        ],
        compiler_params=vmem(12),
    )(stripe, y_factor)
    out = out.reshape(n_var, planes, blocks, rows, rank).transpose(0, 1, 3, 2, 4)
    return out.reshape(n_var, planes, 1, rows, cells)


def solution(mesh):
    n_var, n_gx = mesh.devices.shape
    fine = Mesh(mesh.devices.reshape(n_var // 2, 2, n_gx // 16, 16), (SLOW, CORE, COL, ROW))
    placed = (P(VAR, GX, None, None), P(), P(GX, None), P(), P())
    return jax.shard_map(
        local,
        mesh=fine,
        in_specs=placed,
        out_specs=P(None, None, GX, VAR, None),
        check_vma=False,
    )
```

```python
import functools

import jax
import jax.numpy as jnp
from jax import lax
from jax.experimental import pallas as pl
from jax.experimental.pallas import tpu as pltpu
from jax.sharding import Mesh, PartitionSpec as P

SLOW, CORE, COL, ROW = "var_outer", "var_inner", "gx_outer", "gx_inner"
VAR, GX = (SLOW, CORE), (COL, ROW)
F32, BF16 = jnp.float32, jnp.bfloat16
NT = (((1,), (1,)), ((), ()))
NN = (((1,), (0,)), ((), ()))
VMEM_SPEC = pl.BlockSpec(memory_space=pltpu.VMEM)
HBM_SPEC = pl.BlockSpec(memory_space=pltpu.HBM)


def vmem(mib):
    return pltpu.CompilerParams(vmem_limit_bytes=mib << 20)


def dot(a, b, dims):
    return lax.dot_general(a, b, dims, preferred_element_type=F32)


def pack_kernel(n_slow, core_hbm, mix_hbm, x_hbm, z_hbm, parcel, mix_out, core, mix, xs, zs, sem):
    copies = [
        pltpu.make_async_copy(src, dst, sem.at[i])
        for i, (src, dst) in enumerate([(core_hbm, core), (z_hbm, zs), (x_hbm, xs), (mix_hbm, mix)])
    ]
    for copy in copies:
        copy.start()
    first, planes = core.shape[1], zs.shape[0]
    run = planes // n_slow
    stripe_len, rank = xs.shape
    own = lax.axis_index(SLOW) * first * first + lax.axis_index(CORE)
    index = lax.broadcasted_iota(jnp.int32, (first, stripe_len), 0) * first + own
    picked = (lax.broadcasted_iota(jnp.int32, (first, stripe_len), 1) == index).astype(F32).astype(BF16)
    for copy in copies:
        copy.wait()
    lent = dot(picked, xs[...], NN)
    for d in range(first):
        part = dot(zs[...], core[0, d], NT)
        row = jnp.broadcast_to(lent[d : d + 1], (run, rank))
        for t in range(n_slow):
            start = (t * first + d) * run * 2
            parcel[pl.ds(start, run, stride=2), :] = part[t * run : (t + 1) * run]
            parcel[pl.ds(start + 1, run, stride=2), :] = row
    mix_out[...] = mix[...].astype(F32)


def mix_kernel(n_slow, got, mix, slab, xr):
    n_var = mix.shape[0]
    peers, rank = got.shape[0] // 2, got.shape[1]
    run = peers // n_var
    rows = n_var // n_slow
    weights = mix[...]
    terms = got[pl.ds(0, peers, stride=2), :]
    for v in range(n_var):
        total = None
        for w in range(n_var):
            weight = jnp.broadcast_to(weights[v : v + 1, w : w + 1], (run, rank))
            term = terms[w * run : (w + 1) * run] * weight
            total = term if total is None else total + term
        block = total.astype(BF16)
        for p in range(slab.shape[0]):
            slab[p, v] = block
    half = rank // rows
    to = lax.broadcasted_iota(jnp.int32, (rank, rank), 1)
    source = to % half * rows + to // half
    order = (lax.broadcasted_iota(jnp.int32, (rank, rank), 0) == source).astype(F32).astype(BF16)
    lent = got[pl.ds(1, peers, stride=2), :].astype(BF16)
    lent = dot(lent, order, NN).astype(BF16)
    for t in range(n_slow):
        for s in range(rows):
            start = (t * rows + s) * run
            xr[s, pl.ds(t * run, run)] = lent[start : start + run]


def stripe_kernel(slab, xr, stripe, wide):
    n_row, n_var, share, rank = slab.shape
    rows, peers, _ = xr.shape
    height = n_var * rows
    pitch = wide.shape[0] // peers
    left = xr[...].reshape(rows * peers, rank)
    for v in range(0, n_var, 2):
        right = jnp.concatenate([slab[:, v + d].reshape(n_row * share, rank) for d in range(2)], 1)
        r = dot(left, right, NN)
        for d in range(2):
            for s in range(rows):
                wide[pl.ds((v + d) * rows + s, peers, stride=pitch), :] = r[
                    s * peers : (s + 1) * peers, d * rank : (d + 1) * rank
                ]
    for p in range(peers):
        stripe[p] = wide[pl.ds(p * pitch, height), :].astype(BF16)


def expand_kernel(stripe, y_factor, out, wide, result, packed, sem):
    planes, pairs, rank = stripe.shape
    rows = 2
    n_var = pairs // rows
    blocks = y_factor.shape[0] // rank
    height = blocks * rows
    halves = result.shape[0]
    group = n_var // halves
    lead = wide.shape[0] // planes
    pitch = result.shape[1] // (group * planes)
    for p in range(planes):
        wide[pl.ds(p * lead, pairs), :] = stripe[p].astype(F32)
    copies = []
    for h in range(halves):
        left = jnp.concatenate(
            [
                wide[pl.ds(v * rows + s, planes, stride=lead), :]
                for s in range(rows)
                for v in range(h * group, (h + 1) * group)
            ],
            0,
        ).astype(BF16)
        for c in range(0, blocks, 2):
            r = dot(left, y_factor[pl.ds(c * rank, 2 * rank), :], NT)
            for s in range(rows):
                for d in range(2):
                    result[h, pl.ds((c + d) * rows + s, group * planes, stride=pitch), :] = r[
                        s * group * planes : (s + 1) * group * planes, d * rank : (d + 1) * rank
                    ]
        for j in range(group):
            v = h * group + j
            for p in range(planes):
                piece = result[h, pl.ds((j * planes + p) * pitch, height), :]
                packed[v * planes + p] = piece.astype(BF16)
            copy = pltpu.make_async_copy(
                packed.at[pl.ds(v * planes, planes)], out.at[pl.ds(v * planes, planes)], sem.at[v]
            )
            copy.start()
            copies.append(copy)
    for copy in copies:
        copy.wait()


def local(core, var_mix, x_factor, y_factor, z_factor):
    n_slow, n_core, n_col = lax.axis_size(SLOW), lax.axis_size(CORE), lax.axis_size(COL)
    n_var = n_slow * n_core
    rank = core.shape[3]
    planes, cells = z_factor.shape[0], y_factor.shape[0]
    rows = x_factor.shape[0] // n_var
    assert core.shape[1] == n_core == rows
    peers = planes * n_core
    parcel, mix = pl.pallas_call(
        functools.partial(pack_kernel, n_slow),
        in_specs=[HBM_SPEC] * 4,
        out_specs=[VMEM_SPEC] * 2,
        out_shape=[pltpu.VMEM((peers * 2, rank), F32), pltpu.VMEM(var_mix.shape, F32)],
        scratch_shapes=[
            pltpu.VMEM(core.shape, BF16),
            pltpu.VMEM(var_mix.shape, BF16),
            pltpu.VMEM(x_factor.shape, BF16),
            pltpu.VMEM(z_factor.shape, BF16),
            pltpu.SemaphoreType.DMA((4,)),
        ],
        compiler_params=vmem(4),
    )(*(pltpu.with_memory_space_constraint(a, pltpu.HBM) for a in (core, var_mix, x_factor, z_factor)))
    got = lax.all_to_all(parcel.reshape(peers, 2, rank), (SLOW, CORE, ROW), 0, 0, tiled=True)
    slab, xr = pl.pallas_call(
        functools.partial(mix_kernel, n_slow),
        in_specs=[VMEM_SPEC] * 2,
        out_specs=[VMEM_SPEC] * 2,
        out_shape=[
            jax.ShapeDtypeStruct((n_col, n_var, peers // n_var, rank), BF16),
            jax.ShapeDtypeStruct((rows, planes, rank), BF16),
        ],
        compiler_params=vmem(4),
    )(got.reshape(peers * 2, rank), mix)
    slab = lax.all_to_all(slab, COL, 0, 0, tiled=True)
    slab = lax.all_gather(slab, CORE, tiled=True)
    stripe = pl.pallas_call(
        stripe_kernel,
        in_specs=[VMEM_SPEC] * 2,
        out_specs=VMEM_SPEC,
        out_shape=pltpu.VMEM((planes, n_var * rows, rank), BF16),
        scratch_shapes=[pltpu.VMEM((planes * (n_var * rows + 1), rank), F32)],
        compiler_params=vmem(4),
    )(slab, xr)
    stripe = lax.all_to_all(stripe, (SLOW, ROW), 0, 0, tiled=True)
    blocks = cells // rank
    out = pl.pallas_call(
        expand_kernel,
        in_specs=[VMEM_SPEC] * 2,
        out_specs=HBM_SPEC,
        out_shape=jax.ShapeDtypeStruct((n_var * planes, blocks * rows, rank), BF16),
        scratch_shapes=[
            pltpu.VMEM((planes * (n_var * rows + 1), rank), F32),
            pltpu.VMEM((n_var // 2, 2 * planes * (blocks * rows + 1), rank), F32),
            pltpu.VMEM((n_var * planes, blocks * rows, rank), BF16),
            pltpu.SemaphoreType.DMA((n_var,)),
        ],
        compiler_params=vmem(12),
    )(stripe, y_factor)
    out = out.reshape(n_var, planes, blocks, rows, rank).transpose(0, 1, 3, 2, 4)
    return out.reshape(n_var, planes, 1, rows, cells)


def solution(mesh):
    n_var, n_gx = mesh.devices.shape
    fine = Mesh(mesh.devices.reshape(n_var // 2, 2, n_gx // 16, 16), (SLOW, CORE, COL, ROW))
    placed = (P(VAR, GX, None, None), P(), P(GX, None), P(), P())
    return jax.shard_map(
        local,
        mesh=fine,
        in_specs=placed,
        out_specs=P(None, None, GX, VAR, None),
        check_vma=False,
    )
```

```python
import functools

import jax
import jax.numpy as jnp
from jax import lax
from jax.experimental import pallas as pl
from jax.experimental.pallas import tpu as pltpu
from jax.sharding import Mesh, PartitionSpec as P

SLOW, CORE, COL, ROW = "var_outer", "var_inner", "gx_outer", "gx_inner"
VAR, GX = (SLOW, CORE), (COL, ROW)
F32, BF16 = jnp.float32, jnp.bfloat16
NT = (((1,), (1,)), ((), ()))
NN = (((1,), (0,)), ((), ()))
VMEM_SPEC = pl.BlockSpec(memory_space=pltpu.VMEM)
HBM_SPEC = pl.BlockSpec(memory_space=pltpu.HBM)


def vmem(mib):
    return pltpu.CompilerParams(vmem_limit_bytes=mib << 20)


def dot(a, b, dims):
    return lax.dot_general(a, b, dims, preferred_element_type=F32)


def pack_kernel(n_slow, core_hbm, mix_hbm, x_hbm, z_hbm, parcel, mix_out, core, mix, xs, zs, sem):
    copies = [
        pltpu.make_async_copy(src, dst, sem.at[i])
        for i, (src, dst) in enumerate([(core_hbm, core), (z_hbm, zs), (x_hbm, xs), (mix_hbm, mix)])
    ]
    for copy in copies:
        copy.start()
    first, planes = core.shape[1], zs.shape[0]
    run = planes // n_slow
    stripe_len, rank = xs.shape
    own = lax.axis_index(SLOW) * first * first + lax.axis_index(CORE)
    index = lax.broadcasted_iota(jnp.int32, (first, stripe_len), 0) * first + own
    picked = (lax.broadcasted_iota(jnp.int32, (first, stripe_len), 1) == index).astype(F32).astype(BF16)
    for copy in copies:
        copy.wait()
    lent = dot(picked, xs[...], NN)
    for d in range(first):
        part = dot(zs[...], core[0, d], NT)
        row = jnp.broadcast_to(lent[d : d + 1], (run, rank))
        for t in range(n_slow):
            start = (t * first + d) * run * 2
            parcel[pl.ds(start, run, stride=2), :] = part[t * run : (t + 1) * run]
            parcel[pl.ds(start + 1, run, stride=2), :] = row
    mix_out[...] = mix[...].astype(F32)


def mix_kernel(n_slow, got, mix, slab, xr):
    n_var = mix.shape[0]
    peers, rank = got.shape[0] // 2, got.shape[1]
    run = peers // n_var
    rows = n_var // n_slow
    weights = mix[...]
    terms = got[pl.ds(0, peers, stride=2), :]
    for v in range(n_var):
        total = None
        for w in range(n_var):
            weight = jnp.broadcast_to(weights[v : v + 1, w : w + 1], (run, rank))
            term = terms[w * run : (w + 1) * run] * weight
            total = term if total is None else total + term
        block = total.astype(BF16)
        for p in range(slab.shape[0]):
            slab[p, v] = block
    half = rank // rows
    to = lax.broadcasted_iota(jnp.int32, (rank, rank), 1)
    source = to % half * rows + to // half
    order = (lax.broadcasted_iota(jnp.int32, (rank, rank), 0) == source).astype(F32).astype(BF16)
    lent = got[pl.ds(1, peers, stride=2), :].astype(BF16)
    lent = dot(lent, order, NN).astype(BF16)
    for t in range(n_slow):
        for s in range(rows):
            start = (t * rows + s) * run
            xr[s, pl.ds(t * run, run)] = lent[start : start + run]


def stripe_kernel(slab, xr, stripe, wide):
    n_row, n_var, share, rank = slab.shape
    rows, peers, _ = xr.shape
    height = n_var * rows
    pitch = wide.shape[0] // peers
    left = xr[...].reshape(rows * peers, rank)
    for v in range(0, n_var, 2):
        right = jnp.concatenate([slab[:, v + d].reshape(n_row * share, rank) for d in range(2)], 1)
        r = dot(left, right, NN)
        for d in range(2):
            for s in range(rows):
                wide[pl.ds((v + d) * rows + s, peers, stride=pitch), :] = r[
                    s * peers : (s + 1) * peers, d * rank : (d + 1) * rank
                ]
    for p in range(peers):
        stripe[p] = wide[pl.ds(p * pitch, height), :].astype(BF16)


def expand_kernel(stripe, y_factor, out, wide, result, packed, sem):
    planes, pairs, rank = stripe.shape
    rows = 2
    n_var = pairs // rows
    blocks = y_factor.shape[0] // rank
    height = blocks * rows
    parts = result.shape[0]
    group = n_var // parts
    lead = wide.shape[0] // planes
    pitch = result.shape[1] // (group * planes)
    for p in range(planes):
        wide[pl.ds(p * lead, pairs), :] = stripe[p].astype(F32)
    copies = []

    def pack(h):
        for p in range(group * planes):
            piece = result[h, pl.ds(p * pitch, height), :]
            packed[h * group * planes + p] = piece.astype(BF16)
        span = pl.ds(h * group * planes, group * planes)
        copy = pltpu.make_async_copy(packed.at[span], out.at[span], sem.at[h])
        copy.start()
        copies.append(copy)

    for h in range(parts):
        left = jnp.concatenate(
            [
                wide[pl.ds(v * rows + s, planes, stride=lead), :]
                for s in range(rows)
                for v in range(h * group, (h + 1) * group)
            ],
            0,
        ).astype(BF16)
        for c in range(0, blocks, 2):
            r = dot(left, y_factor[pl.ds(c * rank, 2 * rank), :], NT)
            for s in range(rows):
                for d in range(2):
                    result[h, pl.ds((c + d) * rows + s, group * planes, stride=pitch), :] = r[
                        s * group * planes : (s + 1) * group * planes, d * rank : (d + 1) * rank
                    ]
        if h:
            pack(h - 1)
    pack(parts - 1)
    for copy in copies:
        copy.wait()


def local(core, var_mix, x_factor, y_factor, z_factor):
    n_slow, n_core, n_col = lax.axis_size(SLOW), lax.axis_size(CORE), lax.axis_size(COL)
    n_var = n_slow * n_core
    rank = core.shape[3]
    planes, cells = z_factor.shape[0], y_factor.shape[0]
    rows = x_factor.shape[0] // n_var
    assert core.shape[1] == n_core == rows
    peers = planes * n_core
    parcel, mix = pl.pallas_call(
        functools.partial(pack_kernel, n_slow),
        in_specs=[HBM_SPEC] * 4,
        out_specs=[VMEM_SPEC] * 2,
        out_shape=[pltpu.VMEM((peers * 2, rank), F32), pltpu.VMEM(var_mix.shape, F32)],
        scratch_shapes=[
            pltpu.VMEM(core.shape, BF16),
            pltpu.VMEM(var_mix.shape, BF16),
            pltpu.VMEM(x_factor.shape, BF16),
            pltpu.VMEM(z_factor.shape, BF16),
            pltpu.SemaphoreType.DMA((4,)),
        ],
        compiler_params=vmem(4),
    )(*(pltpu.with_memory_space_constraint(a, pltpu.HBM) for a in (core, var_mix, x_factor, z_factor)))
    got = lax.all_to_all(parcel.reshape(peers, 2, rank), (SLOW, CORE, ROW), 0, 0, tiled=True)
    slab, xr = pl.pallas_call(
        functools.partial(mix_kernel, n_slow),
        in_specs=[VMEM_SPEC] * 2,
        out_specs=[VMEM_SPEC] * 2,
        out_shape=[
            jax.ShapeDtypeStruct((n_core * n_col, n_var, peers // n_var, rank), BF16),
            jax.ShapeDtypeStruct((rows, planes, rank), BF16),
        ],
        compiler_params=vmem(4),
    )(got.reshape(peers * 2, rank), mix)
    slab = lax.all_to_all(slab, (CORE, COL), 0, 0, tiled=True)
    stripe = pl.pallas_call(
        stripe_kernel,
        in_specs=[VMEM_SPEC] * 2,
        out_specs=VMEM_SPEC,
        out_shape=pltpu.VMEM((planes, n_var * rows, rank), BF16),
        scratch_shapes=[pltpu.VMEM((planes * (n_var * rows + 1), rank), F32)],
        compiler_params=vmem(4),
    )(slab, xr)
    stripe = lax.all_to_all(stripe, (SLOW, ROW), 0, 0, tiled=True)
    blocks = cells // rank
    out = pl.pallas_call(
        expand_kernel,
        in_specs=[VMEM_SPEC] * 2,
        out_specs=HBM_SPEC,
        out_shape=jax.ShapeDtypeStruct((n_var * planes, blocks * rows, rank), BF16),
        scratch_shapes=[
            pltpu.VMEM((planes * (n_var * rows + 1), rank), F32),
            pltpu.VMEM((n_var, planes * (blocks * rows + 1), rank), F32),
            pltpu.VMEM((n_var * planes, blocks * rows, rank), BF16),
            pltpu.SemaphoreType.DMA((n_var,)),
        ],
        compiler_params=vmem(12),
    )(stripe, y_factor)
    out = out.reshape(n_var, planes, blocks, rows, rank).transpose(0, 1, 3, 2, 4)
    return out.reshape(n_var, planes, 1, rows, cells)


def solution(mesh):
    n_var, n_gx = mesh.devices.shape
    fine = Mesh(mesh.devices.reshape(n_var // 2, 2, n_gx // 16, 16), (SLOW, CORE, COL, ROW))
    placed = (P(VAR, GX, None, None), P(), P(GX, None), P(), P())
    return jax.shard_map(
        local,
        mesh=fine,
        in_specs=placed,
        out_specs=P(None, None, GX, VAR, None),
        check_vma=False,
    )
```

```python
import functools

import jax
import jax.numpy as jnp
from jax import lax
from jax.experimental import pallas as pl
from jax.experimental.pallas import tpu as pltpu
from jax.sharding import Mesh, PartitionSpec as P

SLOW, CORE, COL, ROW = "var_outer", "var_inner", "gx_outer", "gx_inner"
VAR, GX = (SLOW, CORE), (COL, ROW)
F32, BF16 = jnp.float32, jnp.bfloat16
NT = (((1,), (1,)), ((), ()))
NN = (((1,), (0,)), ((), ()))
VMEM_SPEC = pl.BlockSpec(memory_space=pltpu.VMEM)
HBM_SPEC = pl.BlockSpec(memory_space=pltpu.HBM)


def vmem(mib):
    return pltpu.CompilerParams(vmem_limit_bytes=mib << 20)


def dot(a, b, dims):
    return lax.dot_general(a, b, dims, preferred_element_type=F32)


def pack_kernel(n_slow, core_hbm, mix_hbm, x_hbm, z_hbm, parcel, mix_out, core, mix, xs, zs, sem):
    copies = [
        pltpu.make_async_copy(src, dst, sem.at[i])
        for i, (src, dst) in enumerate([(core_hbm, core), (z_hbm, zs), (x_hbm, xs), (mix_hbm, mix)])
    ]
    for copy in copies:
        copy.start()
    first, planes = core.shape[1], zs.shape[0]
    run = planes // n_slow
    stripe_len, rank = xs.shape
    own = lax.axis_index(SLOW) * first * first + lax.axis_index(CORE)
    index = lax.broadcasted_iota(jnp.int32, (first, stripe_len), 0) * first + own
    picked = (lax.broadcasted_iota(jnp.int32, (first, stripe_len), 1) == index).astype(F32).astype(BF16)
    half = rank // first
    to = lax.broadcasted_iota(jnp.int32, (rank, rank), 1)
    source = to % half * first + to // half
    order = (lax.broadcasted_iota(jnp.int32, (rank, rank), 0) == source).astype(F32).astype(BF16)
    for copy in copies:
        copy.wait()
    lent = dot(dot(picked, xs[...], NN).astype(BF16), order, NN)
    for d in range(first):
        part = dot(zs[...], core[0, d], NT)
        row = jnp.broadcast_to(lent[d : d + 1], (run, rank))
        for t in range(n_slow):
            start = (t * first + d) * run * 2
            parcel[pl.ds(start, run, stride=2), :] = part[t * run : (t + 1) * run]
            parcel[pl.ds(start + 1, run, stride=2), :] = row
    mix_out[...] = mix[...].astype(F32)


def mix_kernel(n_slow, got, mix, slab, xr):
    n_var = mix.shape[0]
    peers, rank = got.shape[0] // 2, got.shape[1]
    run = peers // n_var
    rows = n_var // n_slow
    weights = mix[...]
    terms = got[pl.ds(0, peers, stride=2), :]
    for v in range(n_var):
        total = None
        for w in range(n_var):
            weight = jnp.broadcast_to(weights[v : v + 1, w : w + 1], (run, rank))
            term = terms[w * run : (w + 1) * run] * weight
            total = term if total is None else total + term
        block = total.astype(BF16)
        for p in range(slab.shape[0]):
            slab[p, v] = block
    lent = got[pl.ds(1, peers, stride=2), :].astype(BF16)
    for t in range(n_slow):
        for s in range(rows):
            start = (t * rows + s) * run
            xr[s, pl.ds(t * run, run)] = lent[start : start + run]


def stripe_kernel(slab, xr, stripe, wide):
    n_row, n_var, share, rank = slab.shape
    rows, peers, _ = xr.shape
    height = n_var * rows
    pitch = wide.shape[0] // peers
    left = xr[...].reshape(rows * peers, rank)
    for v in range(0, n_var, 2):
        right = jnp.concatenate([slab[:, v + d].reshape(n_row * share, rank) for d in range(2)], 1)
        r = dot(left, right, NN)
        for d in range(2):
            for s in range(rows):
                wide[pl.ds((v + d) * rows + s, peers, stride=pitch), :] = r[
                    s * peers : (s + 1) * peers, d * rank : (d + 1) * rank
                ]
    for p in range(peers):
        stripe[p] = wide[pl.ds(p * pitch, height), :].astype(BF16)


def expand_kernel(stripe, y_factor, out, wide, result, packed, sem):
    planes, pairs, rank = stripe.shape
    rows = 2
    n_var = pairs // rows
    blocks = y_factor.shape[0] // rank
    height = blocks * rows
    parts = result.shape[0]
    group = n_var // parts
    lead = wide.shape[0] // planes
    pitch = result.shape[1] // (group * planes)
    for p in range(planes):
        wide[pl.ds(p * lead, pairs), :] = stripe[p].astype(F32)
    copies = []

    def pack(h):
        for p in range(group * planes):
            piece = result[h, pl.ds(p * pitch, height), :]
            packed[h * group * planes + p] = piece.astype(BF16)
        span = pl.ds(h * group * planes, group * planes)
        copy = pltpu.make_async_copy(packed.at[span], out.at[span], sem.at[h])
        copy.start()
        copies.append(copy)

    for h in range(parts):
        left = jnp.concatenate(
            [
                wide[pl.ds(v * rows + s, planes, stride=lead), :]
                for s in range(rows)
                for v in range(h * group, (h + 1) * group)
            ],
            0,
        ).astype(BF16)
        for c in range(0, blocks, 2):
            r = dot(left, y_factor[pl.ds(c * rank, 2 * rank), :], NT)
            for s in range(rows):
                for d in range(2):
                    result[h, pl.ds((c + d) * rows + s, group * planes, stride=pitch), :] = r[
                        s * group * planes : (s + 1) * group * planes, d * rank : (d + 1) * rank
                    ]
        if h:
            pack(h - 1)
    pack(parts - 1)
    for copy in copies:
        copy.wait()


def local(core, var_mix, x_factor, y_factor, z_factor):
    n_slow, n_core, n_col = lax.axis_size(SLOW), lax.axis_size(CORE), lax.axis_size(COL)
    n_var = n_slow * n_core
    rank = core.shape[3]
    planes, cells = z_factor.shape[0], y_factor.shape[0]
    rows = x_factor.shape[0] // n_var
    assert core.shape[1] == n_core == rows
    peers = planes * n_core
    parcel, mix = pl.pallas_call(
        functools.partial(pack_kernel, n_slow),
        in_specs=[HBM_SPEC] * 4,
        out_specs=[VMEM_SPEC] * 2,
        out_shape=[pltpu.VMEM((peers * 2, rank), F32), pltpu.VMEM(var_mix.shape, F32)],
        scratch_shapes=[
            pltpu.VMEM(core.shape, BF16),
            pltpu.VMEM(var_mix.shape, BF16),
            pltpu.VMEM(x_factor.shape, BF16),
            pltpu.VMEM(z_factor.shape, BF16),
            pltpu.SemaphoreType.DMA((4,)),
        ],
        compiler_params=vmem(4),
    )(*(pltpu.with_memory_space_constraint(a, pltpu.HBM) for a in (core, var_mix, x_factor, z_factor)))
    got = lax.all_to_all(parcel.reshape(peers, 2, rank), (SLOW, CORE, ROW), 0, 0, tiled=True)
    slab, xr = pl.pallas_call(
        functools.partial(mix_kernel, n_slow),
        in_specs=[VMEM_SPEC] * 2,
        out_specs=[VMEM_SPEC] * 2,
        out_shape=[
            jax.ShapeDtypeStruct((n_core * n_col, n_var, peers // n_var, rank), BF16),
            jax.ShapeDtypeStruct((rows, planes, rank), BF16),
        ],
        compiler_params=vmem(4),
    )(got.reshape(peers * 2, rank), mix)
    slab = lax.all_to_all(slab, (CORE, COL), 0, 0, tiled=True)
    stripe = pl.pallas_call(
        stripe_kernel,
        in_specs=[VMEM_SPEC] * 2,
        out_specs=VMEM_SPEC,
        out_shape=pltpu.VMEM((planes, n_var * rows, rank), BF16),
        scratch_shapes=[pltpu.VMEM((planes * (n_var * rows + 1), rank), F32)],
        compiler_params=vmem(4),
    )(slab, xr)
    stripe = lax.all_to_all(stripe, (SLOW, ROW), 0, 0, tiled=True)
    blocks = cells // rank
    out = pl.pallas_call(
        expand_kernel,
        in_specs=[VMEM_SPEC] * 2,
        out_specs=HBM_SPEC,
        out_shape=jax.ShapeDtypeStruct((n_var * planes, blocks * rows, rank), BF16),
        scratch_shapes=[
            pltpu.VMEM((planes * (n_var * rows + 1), rank), F32),
            pltpu.VMEM((n_var, planes * (blocks * rows + 1), rank), F32),
            pltpu.VMEM((n_var * planes, blocks * rows, rank), BF16),
            pltpu.SemaphoreType.DMA((n_var,)),
        ],
        compiler_params=vmem(12),
    )(stripe, y_factor)
    out = out.reshape(n_var, planes, blocks, rows, rank).transpose(0, 1, 3, 2, 4)
    return out.reshape(n_var, planes, 1, rows, cells)


def solution(mesh):
    n_var, n_gx = mesh.devices.shape
    fine = Mesh(mesh.devices.reshape(n_var // 2, 2, n_gx // 16, 16), (SLOW, CORE, COL, ROW))
    placed = (P(VAR, GX, None, None), P(), P(GX, None), P(), P())
    return jax.shard_map(
        local,
        mesh=fine,
        in_specs=placed,
        out_specs=P(None, None, GX, VAR, None),
        check_vma=False,
    )
```

```python
import functools

import jax
import jax.numpy as jnp
from jax import lax
from jax.experimental import pallas as pl
from jax.experimental.pallas import tpu as pltpu
from jax.sharding import Mesh, PartitionSpec as P

SLOW, CORE, COL, ROW = "var_outer", "var_inner", "gx_outer", "gx_inner"
VAR, GX = (SLOW, CORE), (COL, ROW)
F32, BF16 = jnp.float32, jnp.bfloat16
NT = (((1,), (1,)), ((), ()))
NN = (((1,), (0,)), ((), ()))
VMEM_SPEC = pl.BlockSpec(memory_space=pltpu.VMEM)
HBM_SPEC = pl.BlockSpec(memory_space=pltpu.HBM)


def vmem(mib):
    return pltpu.CompilerParams(vmem_limit_bytes=mib << 20)


def dot(a, b, dims):
    return lax.dot_general(a, b, dims, preferred_element_type=F32)


def pack_kernel(n_slow, core_hbm, mix_hbm, x_hbm, z_hbm, parcel, mix_out, core, mix, xs, zs, sem):
    copies = [
        pltpu.make_async_copy(src, dst, sem.at[i])
        for i, (src, dst) in enumerate([(core_hbm, core), (z_hbm, zs), (x_hbm, xs), (mix_hbm, mix)])
    ]
    for copy in copies:
        copy.start()
    first, planes = core.shape[1], zs.shape[0]
    run = planes // n_slow
    stripe_len, rank = xs.shape
    own = lax.axis_index(SLOW) * first * first + lax.axis_index(CORE)
    index = lax.broadcasted_iota(jnp.int32, (first, stripe_len), 0) * first + own
    picked = (lax.broadcasted_iota(jnp.int32, (first, stripe_len), 1) == index).astype(F32).astype(BF16)
    for copy in copies:
        copy.wait()
    lent = dot(picked, xs[...], NN)
    for d in range(first):
        part = dot(zs[...], core[0, d], NT)
        row = jnp.broadcast_to(lent[d : d + 1], (run, rank))
        for t in range(n_slow):
            start = (t * first + d) * run * 2
            parcel[pl.ds(start, run, stride=2), :] = part[t * run : (t + 1) * run]
            parcel[pl.ds(start + 1, run, stride=2), :] = row
    mix_out[...] = mix[...].astype(F32)


def mix_kernel(n_slow, got, mix, slab, xr):
    n_var = mix.shape[0]
    peers, rank = got.shape[0] // 2, got.shape[1]
    run = peers // n_var
    rows = n_var // n_slow
    weights = mix[...]
    terms = got[pl.ds(0, peers, stride=2), :]
    for v in range(n_var):
        total = None
        for w in range(n_var):
            weight = jnp.broadcast_to(weights[v : v + 1, w : w + 1], (run, rank))
            term = terms[w * run : (w + 1) * run] * weight
            total = term if total is None else total + term
        block = total.astype(BF16)
        for p in range(slab.shape[0]):
            slab[p, v] = block
    to = lax.broadcasted_iota(jnp.int32, (rank, rank), 1)
    source = (to // (run * rows) * run + to % run) * rows + to // run % rows
    order = (lax.broadcasted_iota(jnp.int32, (rank, rank), 0) == source).astype(F32).astype(BF16)
    lent = got[pl.ds(1, peers, stride=2), :].astype(BF16)
    lent = dot(lent, order, NN).astype(BF16)
    for t in range(n_slow):
        for s in range(rows):
            start = (t * rows + s) * run
            xr[s, pl.ds(t * run, run)] = lent[start : start + run]


def stripe_kernel(slab, xr, stripe, wide):
    n_row, n_var, share, rank = slab.shape
    rows, peers, _ = xr.shape
    height = n_var * rows
    pitch = wide.shape[0] // peers
    left = xr[...].reshape(rows * peers, rank)
    for v in range(0, n_var, 2):
        right = jnp.concatenate([slab[:, v + d].reshape(n_row * share, rank) for d in range(2)], 1)
        r = dot(left, right, NN)
        for d in range(2):
            for s in range(rows):
                wide[pl.ds((v + d) * rows + s, peers, stride=pitch), :] = r[
                    s * peers : (s + 1) * peers, d * rank : (d + 1) * rank
                ]
    for p in range(peers):
        stripe[p] = wide[pl.ds(p * pitch, height), :].astype(BF16)


def expand_kernel(stripe, y_factor, out, wide, result, packed, sem):
    planes, pairs, rank = stripe.shape
    rows = 2
    n_var = pairs // rows
    blocks = y_factor.shape[0] // rank
    height = blocks * rows
    parts = result.shape[0]
    group = n_var // parts
    lead = wide.shape[0] // planes
    pitch = result.shape[1] // (group * planes)
    for p in range(planes):
        wide[pl.ds(p * lead, pairs), :] = stripe[p].astype(F32)
    copies = []

    def pack(h):
        for p in range(group * planes):
            piece = result[h, pl.ds(p * pitch, height), :]
            packed[h * group * planes + p] = piece.astype(BF16)
        span = pl.ds(h * group * planes, group * planes)
        copy = pltpu.make_async_copy(packed.at[span], out.at[span], sem.at[h])
        copy.start()
        copies.append(copy)

    for h in range(parts):
        left = jnp.concatenate(
            [
                wide[pl.ds(v * rows + s, planes, stride=lead), :]
                for s in range(rows)
                for v in range(h * group, (h + 1) * group)
            ],
            0,
        ).astype(BF16)
        for c in range(0, blocks, 2):
            r = dot(left, y_factor[pl.ds(c * rank, 2 * rank), :], NT)
            for s in range(rows):
                for d in range(2):
                    result[h, pl.ds((c + d) * rows + s, group * planes, stride=pitch), :] = r[
                        s * group * planes : (s + 1) * group * planes, d * rank : (d + 1) * rank
                    ]
        if h:
            pack(h - 1)
    pack(parts - 1)
    for copy in copies:
        copy.wait()


def local(core, var_mix, x_factor, y_factor, z_factor):
    n_slow, n_core, n_col = lax.axis_size(SLOW), lax.axis_size(CORE), lax.axis_size(COL)
    n_var = n_slow * n_core
    rank = core.shape[3]
    planes, cells = z_factor.shape[0], y_factor.shape[0]
    rows = x_factor.shape[0] // n_var
    assert core.shape[1] == n_core == rows
    peers = planes * n_core
    parcel, mix = pl.pallas_call(
        functools.partial(pack_kernel, n_slow),
        in_specs=[HBM_SPEC] * 4,
        out_specs=[VMEM_SPEC] * 2,
        out_shape=[pltpu.VMEM((peers * 2, rank), F32), pltpu.VMEM(var_mix.shape, F32)],
        scratch_shapes=[
            pltpu.VMEM(core.shape, BF16),
            pltpu.VMEM(var_mix.shape, BF16),
            pltpu.VMEM(x_factor.shape, BF16),
            pltpu.VMEM(z_factor.shape, BF16),
            pltpu.SemaphoreType.DMA((4,)),
        ],
        compiler_params=vmem(4),
    )(*(pltpu.with_memory_space_constraint(a, pltpu.HBM) for a in (core, var_mix, x_factor, z_factor)))
    got = lax.all_to_all(parcel.reshape(peers, 2, rank), (SLOW, CORE, ROW), 0, 0, tiled=True)
    slab, xr = pl.pallas_call(
        functools.partial(mix_kernel, n_slow),
        in_specs=[VMEM_SPEC] * 2,
        out_specs=[VMEM_SPEC] * 2,
        out_shape=[
            jax.ShapeDtypeStruct((n_core * n_col, n_var, peers // n_var, rank), BF16),
            jax.ShapeDtypeStruct((rows, planes, rank), BF16),
        ],
        compiler_params=vmem(4),
    )(got.reshape(peers * 2, rank), mix)
    slab = lax.all_to_all(slab, (COL, CORE), 0, 0, tiled=True)
    stripe = pl.pallas_call(
        stripe_kernel,
        in_specs=[VMEM_SPEC] * 2,
        out_specs=VMEM_SPEC,
        out_shape=pltpu.VMEM((planes, n_var * rows, rank), BF16),
        scratch_shapes=[pltpu.VMEM((planes * (n_var * rows + 1), rank), F32)],
        compiler_params=vmem(4),
    )(slab, xr)
    stripe = lax.all_to_all(stripe, (SLOW, ROW), 0, 0, tiled=True)
    blocks = cells // rank
    out = pl.pallas_call(
        expand_kernel,
        in_specs=[VMEM_SPEC] * 2,
        out_specs=HBM_SPEC,
        out_shape=jax.ShapeDtypeStruct((n_var * planes, blocks * rows, rank), BF16),
        scratch_shapes=[
            pltpu.VMEM((planes * (n_var * rows + 1), rank), F32),
            pltpu.VMEM((n_var, planes * (blocks * rows + 1), rank), F32),
            pltpu.VMEM((n_var * planes, blocks * rows, rank), BF16),
            pltpu.SemaphoreType.DMA((n_var,)),
        ],
        compiler_params=vmem(12),
    )(stripe, y_factor)
    out = out.reshape(n_var, planes, blocks, rows, rank).transpose(0, 1, 3, 2, 4)
    return out.reshape(n_var, planes, 1, rows, cells)


def solution(mesh):
    n_var, n_gx = mesh.devices.shape
    fine = Mesh(mesh.devices.reshape(n_var // 2, 2, n_gx // 16, 16), (SLOW, CORE, COL, ROW))
    placed = (P(VAR, GX, None, None), P(), P(GX, None), P(), P())
    return jax.shard_map(
        local,
        mesh=fine,
        in_specs=placed,
        out_specs=P(None, None, GX, VAR, None),
        check_vma=False,
    )
```

```python
import functools

import jax
import jax.numpy as jnp
from jax import lax
from jax.experimental import pallas as pl
from jax.experimental.pallas import tpu as pltpu
from jax.sharding import Mesh, PartitionSpec as P

SLOW, CORE, COL, ROW = "var_outer", "var_inner", "gx_outer", "gx_inner"
VAR, GX = (SLOW, CORE), (COL, ROW)
F32, BF16 = jnp.float32, jnp.bfloat16
NT = (((1,), (1,)), ((), ()))
NN = (((1,), (0,)), ((), ()))
VMEM_SPEC = pl.BlockSpec(memory_space=pltpu.VMEM)
HBM_SPEC = pl.BlockSpec(memory_space=pltpu.HBM)


def vmem(mib):
    return pltpu.CompilerParams(vmem_limit_bytes=mib << 20)


def dot(a, b, dims):
    return lax.dot_general(a, b, dims, preferred_element_type=F32)


def pack_kernel(n_slow, core_hbm, mix_hbm, x_hbm, z_hbm, parcel, mix_out, core, mix, xs, zs, sem):
    copies = [
        pltpu.make_async_copy(src, dst, sem.at[i])
        for i, (src, dst) in enumerate([(core_hbm, core), (z_hbm, zs), (x_hbm, xs), (mix_hbm, mix)])
    ]
    for copy in copies:
        copy.start()
    first, planes = core.shape[1], zs.shape[0]
    run = planes // n_slow
    stripe_len, rank = xs.shape
    own = lax.axis_index(SLOW) * first * first + lax.axis_index(CORE)
    index = lax.broadcasted_iota(jnp.int32, (first, stripe_len), 0) * first + own
    picked = (lax.broadcasted_iota(jnp.int32, (first, stripe_len), 1) == index).astype(F32).astype(BF16)
    for copy in copies:
        copy.wait()
    lent = dot(picked, xs[...], NN)
    for d in range(first):
        part = dot(zs[...], core[0, d], NT)
        row = jnp.broadcast_to(lent[d : d + 1], (run, rank))
        for t in range(n_slow):
            start = (t * first + d) * run * 2
            parcel[pl.ds(start, run, stride=2), :] = part[t * run : (t + 1) * run]
            parcel[pl.ds(start + 1, run, stride=2), :] = row
    mix_out[...] = mix[...].astype(F32)


def mix_kernel(n_slow, got, mix, slab, xr):
    n_var = mix.shape[0]
    peers, rank = got.shape[0] // 2, got.shape[1]
    run = peers // n_var
    rows = n_var // n_slow
    weights = mix[...]
    terms = got[pl.ds(0, peers, stride=2), :]
    for v in range(n_var):
        total = None
        for w in range(n_var):
            weight = jnp.broadcast_to(weights[v : v + 1, w : w + 1], (run, rank))
            term = terms[w * run : (w + 1) * run] * weight
            total = term if total is None else total + term
        block = total.astype(BF16)
        for p in range(slab.shape[0]):
            slab[p, v] = block
    to = lax.broadcasted_iota(jnp.int32, (rank, rank), 1)
    source = (to // (run * rows) * run + to % run) * rows + to // run % rows
    order = (lax.broadcasted_iota(jnp.int32, (rank, rank), 0) == source).astype(F32).astype(BF16)
    lent = got[pl.ds(1, peers, stride=2), :].astype(BF16)
    lent = dot(lent, order, NN).astype(BF16)
    for t in range(n_slow):
        for s in range(rows):
            start = (t * rows + s) * run
            xr[s, pl.ds(t * run, run)] = lent[start : start + run]


def stripe_kernel(slab, xr, stripe, wide):
    n_row, n_var, share, rank = slab.shape
    rows, peers, _ = xr.shape
    height = n_var * rows
    pitch = wide.shape[0] // peers
    left = xr[...].reshape(rows * peers, rank)
    for v in range(0, n_var, 4):
        right = jnp.concatenate([slab[:, v + d].reshape(n_row * share, rank) for d in range(4)], 1)
        r = dot(left, right, NN)
        for d in range(4):
            for s in range(rows):
                wide[pl.ds((v + d) * rows + s, peers, stride=pitch), :] = r[
                    s * peers : (s + 1) * peers, d * rank : (d + 1) * rank
                ]
    for p in range(peers):
        stripe[p] = wide[pl.ds(p * pitch, height), :].astype(BF16)


def expand_kernel(stripe, y_factor, out, wide, result, packed, sem):
    planes, pairs, rank = stripe.shape
    rows = 2
    n_var = pairs // rows
    blocks = y_factor.shape[0] // rank
    height = blocks * rows
    parts = result.shape[0]
    group = n_var // parts
    lead = wide.shape[0] // planes
    pitch = result.shape[1] // (group * planes)
    for p in range(planes):
        wide[pl.ds(p * lead, pairs), :] = stripe[p].astype(F32)
    copies = []

    def pack(h):
        for p in range(group * planes):
            piece = result[h, pl.ds(p * pitch, height), :]
            packed[h * group * planes + p] = piece.astype(BF16)
        span = pl.ds(h * group * planes, group * planes)
        copy = pltpu.make_async_copy(packed.at[span], out.at[span], sem.at[h])
        copy.start()
        copies.append(copy)

    for h in range(parts):
        left = jnp.concatenate(
            [
                wide[pl.ds(v * rows + s, planes, stride=lead), :]
                for s in range(rows)
                for v in range(h * group, (h + 1) * group)
            ],
            0,
        ).astype(BF16)
        for c in range(0, blocks, 2):
            r = dot(left, y_factor[pl.ds(c * rank, 2 * rank), :], NT)
            for s in range(rows):
                for d in range(2):
                    result[h, pl.ds((c + d) * rows + s, group * planes, stride=pitch), :] = r[
                        s * group * planes : (s + 1) * group * planes, d * rank : (d + 1) * rank
                    ]
        if h:
            pack(h - 1)
    pack(parts - 1)
    for copy in copies:
        copy.wait()


def local(core, var_mix, x_factor, y_factor, z_factor):
    n_slow, n_core, n_col = lax.axis_size(SLOW), lax.axis_size(CORE), lax.axis_size(COL)
    n_var = n_slow * n_core
    rank = core.shape[3]
    planes, cells = z_factor.shape[0], y_factor.shape[0]
    rows = x_factor.shape[0] // n_var
    assert core.shape[1] == n_core == rows
    peers = planes * n_core
    parcel, mix = pl.pallas_call(
        functools.partial(pack_kernel, n_slow),
        in_specs=[HBM_SPEC] * 4,
        out_specs=[VMEM_SPEC] * 2,
        out_shape=[pltpu.VMEM((peers * 2, rank), F32), pltpu.VMEM(var_mix.shape, F32)],
        scratch_shapes=[
            pltpu.VMEM(core.shape, BF16),
            pltpu.VMEM(var_mix.shape, BF16),
            pltpu.VMEM(x_factor.shape, BF16),
            pltpu.VMEM(z_factor.shape, BF16),
            pltpu.SemaphoreType.DMA((4,)),
        ],
        compiler_params=vmem(4),
    )(*(pltpu.with_memory_space_constraint(a, pltpu.HBM) for a in (core, var_mix, x_factor, z_factor)))
    got = lax.all_to_all(parcel.reshape(peers, 2, rank), (SLOW, CORE, ROW), 0, 0, tiled=True)
    slab, xr = pl.pallas_call(
        functools.partial(mix_kernel, n_slow),
        in_specs=[VMEM_SPEC] * 2,
        out_specs=[VMEM_SPEC] * 2,
        out_shape=[
            jax.ShapeDtypeStruct((n_core * n_col, n_var, peers // n_var, rank), BF16),
            jax.ShapeDtypeStruct((rows, planes, rank), BF16),
        ],
        compiler_params=vmem(4),
    )(got.reshape(peers * 2, rank), mix)
    slab = lax.all_to_all(slab, (COL, CORE), 0, 0, tiled=True)
    stripe = pl.pallas_call(
        stripe_kernel,
        in_specs=[VMEM_SPEC] * 2,
        out_specs=VMEM_SPEC,
        out_shape=pltpu.VMEM((planes, n_var * rows, rank), BF16),
        scratch_shapes=[pltpu.VMEM((planes * (n_var * rows + 1), rank), F32)],
        compiler_params=vmem(4),
    )(slab, xr)
    stripe = lax.all_to_all(stripe, (SLOW, ROW), 0, 0, tiled=True)
    blocks = cells // rank
    out = pl.pallas_call(
        expand_kernel,
        in_specs=[VMEM_SPEC] * 2,
        out_specs=HBM_SPEC,
        out_shape=jax.ShapeDtypeStruct((n_var * planes, blocks * rows, rank), BF16),
        scratch_shapes=[
            pltpu.VMEM((planes * (n_var * rows + 1), rank), F32),
            pltpu.VMEM((n_var, planes * (blocks * rows + 1), rank), F32),
            pltpu.VMEM((n_var * planes, blocks * rows, rank), BF16),
            pltpu.SemaphoreType.DMA((n_var,)),
        ],
        compiler_params=vmem(12),
    )(stripe, y_factor)
    out = out.reshape(n_var, planes, blocks, rows, rank).transpose(0, 1, 3, 2, 4)
    return out.reshape(n_var, planes, 1, rows, cells)


def solution(mesh):
    n_var, n_gx = mesh.devices.shape
    fine = Mesh(mesh.devices.reshape(n_var // 2, 2, n_gx // 16, 16), (SLOW, CORE, COL, ROW))
    placed = (P(VAR, GX, None, None), P(), P(GX, None), P(), P())
    return jax.shard_map(
        local,
        mesh=fine,
        in_specs=placed,
        out_specs=P(None, None, GX, VAR, None),
        check_vma=False,
    )
```
